128 devices in a mesh: section: 4 (over x), dp: 32 (over y, z, core).
Axes of the slice: x: 4, y: 4, z: 4, core: 2. Of those that a mesh axis runs over, the one named last changes fastest.
Arguments:
- hidden_acts: bfloat16 [4, 4096, 28672], P('section', 'dp'), may hold values from -6 to 6
- layer_inputs: bfloat16 [4, 4096, 8192], P('section', 'dp'), may hold values from -20 to 20
- norm_gains: bfloat16 [4, 8192], P('section'), may hold values from 0.099609375 to 0.59765625
- top_cotangent: bfloat16 [4096, 8192], P('dp'), may hold values from -6 to 6
- up_factors: bfloat16 [32, 4, 32, 28672], P('dp', 'section'), may hold values from -0.005859375 to 0.005859375
- down_factors: bfloat16 [32, 4, 32, 8192], P('dp', 'section'), may hold values from -0.0625 to 0.0625
- candidates: int32 [32, 8], replicated, may hold values from 0 to 31, all different within a row; in each aligned block of 32 rows (0 to 31, 32 to 63, ...) at most 10 rows name the same one
- counts: int32 [32], P('dp'), may hold values from 1 to 128, 3072 in all
Outputs:
- scores: float32 [4, 4096, 32], P('section', 'dp')
The draws below stay inside these ranges and needn't reach their ends.
Inputs may be any that keep to these rules, and one draw needn't show every extreme that they name: `candidates`: each row lists 8 different shards; every shard is listed by at most 10 queries, a bound that some block reaches.
All inputs are finite; a program needn't handle non-finite values. No bound on the sum of `counts` on one device may be relied on, other than what follows from the above.
Results may differ from the reference program's by a relative error of at most 0.0029.
Values may be sent and summed in bfloat16 or wider, within the bound.
No kernel may reach another device: no remote copies, remote signals or barrier semaphores. Data moves between devices by JAX's collectives and lax.ppermute only.
A program may use at most 192 MiB of HBM per device.

```python
import math
import jax
import jax.numpy as jnp
import numpy as np
from jax import lax

D = 8192
FF = 28672
R = 32
TOK_DEV = 128
SECTIONS = 4
QUERIES = 32
CANDS = 8
CAP = 10
TOKENS = 4096
N_DP = 32


def draw_layer_inputs(key, part):
    key = jax.random.fold_in(key, 11)
    base_key, scale_key = jax.random.split(key)
    scales = jnp.exp(jax.random.uniform(scale_key, (SECTIONS, TOKENS, 1), jnp.float32, math.log(0.3), math.log(3.0)))
    base = jax.random.normal(base_key, (SECTIONS, TOKENS, D), jnp.float32)
    return jnp.clip(base * scales, -20.0, 20.0).astype(jnp.bfloat16)


def block_levels(own_key, shape, pieces, low, largest):
    factor_of, own = 1.0, jax.random.fold_in(own_key, 6)
    for dim, parts in pieces:
        steps = jnp.exp(jax.random.uniform(jax.random.fold_in(own, dim), (parts,), jnp.float32, low / len(pieces), largest / len(pieces)))
        factor_of = factor_of * jnp.repeat(steps, shape[dim] // parts).reshape([-1 if axis == dim else 1 for axis in range(len(shape))])
    return factor_of


def split_up(count, total, bound, skew):
    loads = [(1 << 20) // math.isqrt(standing ** skew) + 1 for standing in range(2, count + 1)]
    rest, given = total - bound - (count - 1), [1] * (count - 1)
    while rest > 0:
        movable = [i for i in range(count - 1) if given[i] < bound]
        whole, remaining = sum([loads[i] for i in movable]), rest
        for i in movable:
            extra = min(bound - given[i], max(1, remaining * loads[i] // whole), rest)
            given[i] = given[i] + extra
            rest = rest - extra
    return np.array([bound] + given)


def ragged_sizes(rng, amount, total, bound, lean):
    if amount == 2:
        one = jax.random.randint(rng, (), max(1, total - bound), min(bound, total - 1) + 1)
        return jnp.stack([one, total - one])
    tallies = jnp.asarray(split_up(amount, total, bound, lean), jnp.int32)
    pairs = (amount - 1) // 2
    donor, receiver = tallies[1:1 + 2 * pairs:2], tallies[2:2 + 2 * pairs:2]
    margin = jnp.minimum(donor - 1, bound - receiver)
    moved = jax.random.randint(jax.random.fold_in(rng, 1), (pairs,), 0, 1 << 20) % (margin + 1)
    tallies = tallies.at[1:1 + 2 * pairs:2].set(donor - moved).at[2:2 + 2 * pairs:2].set(receiver + moved)
    return tallies[jax.random.permutation(jax.random.fold_in(rng, 2), amount)]


def deal_out(stream_key, own, number, rows, amount, top, limit, lean):
    ranking = jax.random.permutation(stream_key, amount)
    crowded, common = load_shares(amount, rows * top, limit, lean, True), load_shares(amount, rows * top, limit, lean, False)
    places = jnp.arange(amount)

    def named(lengths, offset_by):
        used = int((lengths > 0).sum())
        fixed = max(1, used // 4)
        moved = fixed + (places - fixed + offset_by * (used - fixed)) % max(1, amount - fixed)
        return jnp.zeros((amount,), jnp.int32).at[ranking[jnp.where(places < fixed, places, moved)]].set(jnp.asarray(lengths, jnp.int32))

    lengths = jnp.where(number % 4 == 0, named(crowded, number // 4), named(common, number - number // 4 - 1))
    mixed = jax.random.permutation(jax.random.fold_in(own, 3), amount)
    donor, receiver = mixed[0:amount // 2 * 2:2], mixed[1:amount // 2 * 2:2]
    margin = jnp.minimum(lengths[donor] - 1, limit - lengths[receiver]) // 2
    margin = jnp.where((donor == ranking[0]) | (receiver == ranking[0]) | (lengths[receiver] == 0), 0, jnp.maximum(margin, 0))
    moved = jax.random.randint(jax.random.fold_in(own, 4), (amount // 2,), 0, 1 << 20) % (margin + 1)
    lengths = lengths.at[donor].add(-moved).at[receiver].add(moved)
    labels = jnp.searchsorted(jnp.cumsum(lengths), jnp.arange(rows * top), side="right").astype(jnp.int32)
    grid = labels.reshape(top, rows).T
    grid = grid[jax.random.permutation(jax.random.fold_in(own, 1), rows)]
    offset_by = jax.random.randint(jax.random.fold_in(own, 2), (rows, 1), 0, top)
    return jnp.take_along_axis(grid, (jnp.arange(top)[None, :] + offset_by) % top, axis=1)


def load_shares(amount, total, bound, skew, full):
    weights = [(1 << 20) // math.isqrt(rank ** skew) + 1 for rank in range(1, amount + 1)]
    largest = bound if full else min(bound, max(-(-total // amount), total * weights[0] // sum(weights)))
    least = 1 if total - largest >= amount - 1 else 0
    given, rest = [largest] + [least] * (amount - 1), total - largest - least * (amount - 1)
    while rest > 0:
        free = [i for i in range(1, amount) if given[i] < largest] or [i for i in range(1, amount) if given[i] < bound]
        mass, budget = sum([weights[i] for i in free]), rest
        for i in free:
            addition = min(bound - given[i], max(1, budget * weights[i] // mass), rest)
            given[i] = given[i] + addition
            rest = rest - addition
    return np.array(given)


def normal_values(rng, extent, deviation, bound, cuts=(), kind=jnp.bfloat16):
    factor_of = block_levels(rng, extent, cuts, -0.22, 0.18) if cuts else 1.0
    array = jax.random.normal(rng, extent, jnp.float32) * deviation * factor_of
    return jnp.minimum(jnp.maximum(array, -bound), bound).astype(kind)


def setup_inputs(seed: int = 0) -> dict:
    key_list = jax.random.split(jax.random.key(seed), 9)
    hidden_acts = normal_values(key_list[0], (SECTIONS, TOKENS, FF), 1.0, 6.0, ((0, 4), (1, 32)))
    layer_inputs = draw_layer_inputs(jax.random.fold_in(key_list[8], 71), 0)
    norm_gains = jnp.clip(jnp.exp(math.log(0.59765625) - 1.7917595 * jax.random.uniform(key_list[2], (SECTIONS, D), jnp.float32) ** block_levels(key_list[2], (SECTIONS, D), ((0, 4),), -0.2, 0.2)), 0.099609375, 0.59765625).astype(jnp.bfloat16)
    top_cotangent = normal_values(key_list[3], (TOKENS, D), 1.0, 6.0, ((0, 32),))
    up_factors = normal_values(key_list[4], (QUERIES, SECTIONS, R, FF), (FF * R) ** -0.5, 0.005859375, ((0, 32), (1, 4)))
    down_factors = normal_values(key_list[5], (QUERIES, SECTIONS, R, D), D ** -0.5, 0.0625, ((0, 32), (1, 4)))
    candidates_keys = jax.random.split(jax.random.fold_in(key_list[6], 1), QUERIES // QUERIES)
    candidates_turns = jax.random.permutation(jax.random.fold_in(key_list[6], 3), QUERIES // QUERIES)
    candidates = jax.vmap(lambda own, number: deal_out(jax.random.fold_in(key_list[6], 2), own, number, QUERIES, N_DP, CANDS, CAP, 2))(candidates_keys, candidates_turns).reshape((QUERIES, CANDS))
    counts = ragged_sizes(key_list[7], N_DP, N_DP * TOK_DEV * 3 // 4, TOK_DEV, 2).astype(jnp.int32)
    return {"hidden_acts": hidden_acts, "layer_inputs": layer_inputs, "norm_gains": norm_gains, "top_cotangent": top_cotangent, "up_factors": up_factors, "down_factors": down_factors, "candidates": candidates, "counts": counts}


EPSILON = 1e-05

def norm_terms(inputs):
    values = inputs.astype(jnp.float32)
    inverse = lax.rsqrt(lax.optimization_barrier(jnp.mean(values * values, axis=-1, keepdims=True)) + EPSILON)
    return (values * inverse, inverse)

def transition(cotangent, normed, inverse, gain_row):
    scaled = gain_row * cotangent
    return cotangent + scaled * inverse - normed * inverse * lax.optimization_barrier(jnp.mean(normed * scaled, axis=-1, keepdims=True))

def reference(hidden_acts, layer_inputs, norm_gains, top_cotangent, up_factors, down_factors, candidates, counts):
    sections = hidden_acts.shape[0]
    shards = counts.shape[0]
    queries = candidates.shape[0]
    rows = hidden_acts.shape[1] // shards
    cotangents = [None] * sections
    cotangent = top_cotangent.astype(jnp.float32)
    cotangents[sections - 1] = cotangent
    for layer in range(sections - 1, 0, -1):
        normed, inverse = norm_terms(layer_inputs[layer])
        cotangent = transition(cotangent, normed, inverse, norm_gains[layer].astype(jnp.float32)[None, :])
        cotangents[layer - 1] = cotangent
    live_rows = (jnp.arange(rows, dtype=jnp.int32)[None, :] < counts[:, None]).astype(jnp.float32)
    outputs = []
    for layer in range(sections):
        hidden_blocks = hidden_acts[layer].reshape(shards, rows, -1)
        cot_blocks = cotangents[layer].astype(jnp.bfloat16).reshape(shards, rows, -1)
        up_layer = up_factors[:, layer]
        down_layer = down_factors[:, layer]

        def one_query(carry, query, hidden_blocks=hidden_blocks, cot_blocks=cot_blocks, up_layer=up_layer, down_layer=down_layer):
            chosen = candidates[query]
            hidden_sel = hidden_blocks[chosen].astype(jnp.float32)
            cot_sel = cot_blocks[chosen].astype(jnp.float32)
            proj_up = jnp.einsum('ktf,rf->ktr', hidden_sel, up_layer[query].astype(jnp.float32), precision=lax.Precision.HIGHEST)
            proj_down = jnp.einsum('ktd,rd->ktr', cot_sel, down_layer[query].astype(jnp.float32), precision=lax.Precision.HIGHEST)
            return (carry.at[chosen, :, query].set(lax.optimization_barrier(jnp.sum(proj_up * proj_down, axis=-1))), None)
        dense, unused = lax.scan(one_query, jnp.zeros((shards, rows, queries), jnp.float32), jnp.arange(queries, dtype=jnp.int32))
        outputs.append((dense * live_rows[:, :, None]).reshape(shards * rows, queries))
    return jnp.stack(outputs)
```

```python
import functools

import jax
import jax.numpy as jnp
from jax import lax
from jax.experimental import pallas as pl
from jax.experimental.pallas import tpu as pltpu
from jax.sharding import PartitionSpec as P

EPSILON = 1e-05
SIDE = 4
CORES = 2
RELATIVE = (0, 3, 1, 2)


def device_id(y, z, c):
    return ((y % SIDE) * SIDE + z % SIDE) * CORES + c % CORES


def shifted(block, dy=0, dz=0, dc=0):
    route = [
        (device_id(y, z, c), device_id(y + dy, z + dz, c + dc))
        for y in range(SIDE)
        for z in range(SIDE)
        for c in range(CORES)
    ]
    return lax.ppermute(block, "dp", route)


def chain_kernel(inputs_ref, gains_ref, top_ref, out_ref):
    sections = inputs_ref.shape[0]
    out_ref[sections - 1] = top_ref[...]
    cotangent = top_ref[...].astype(jnp.float32)
    for layer in range(sections - 1, 0, -1):
        values = inputs_ref[layer].astype(jnp.float32)
        inverse = lax.rsqrt(jnp.mean(values * values, axis=-1, keepdims=True) + EPSILON)
        normed = values * inverse
        scaled = gains_ref[layer : layer + 1, :].astype(jnp.float32) * cotangent
        pulled = jnp.mean(normed * scaled, axis=-1, keepdims=True)
        cotangent = cotangent + scaled * inverse - normed * inverse * pulled
        out_ref[layer - 1] = cotangent.astype(out_ref.dtype)


def chain(inputs, gains, top):
    sections, rows, width = inputs.shape
    step = 16
    return pl.pallas_call(
        chain_kernel,
        grid=(rows // step,),
        in_specs=[
            pl.BlockSpec((sections, step, width), lambda i: (0, i, 0)),
            pl.BlockSpec((sections, width), lambda i: (0, 0)),
            pl.BlockSpec((step, width), lambda i: (i, 0)),
        ],
        out_specs=pl.BlockSpec((sections, step, width), lambda i: (0, i, 0)),
        out_shape=jax.ShapeDtypeStruct(inputs.shape, jnp.bfloat16),
        compiler_params=pltpu.CompilerParams(vmem_limit_bytes=48 << 20),
        cost_estimate=pl.CostEstimate(
            flops=40 * rows * width, bytes_accessed=18 * rows * width, transcendentals=0
        ),
        name="cotangent_chain",
    )(inputs, gains, top)


def proj_kernel(capacity, where_ref, tokens_ref, *refs):
    del where_ref
    factor_refs, out_ref, total_ref = refs[:capacity], refs[capacity], refs[capacity + 1]
    step = pl.program_id(0)
    factors = jnp.concatenate([ref[0] for ref in factor_refs], axis=0)
    part = lax.dot_general(
        factors, tokens_ref[...], (((1,), (1,)), ((), ())), preferred_element_type=jnp.float32
    )

    @pl.when(step == 0)
    def _():
        total_ref[...] = part

    @pl.when(step > 0)
    def _():
        total_ref[...] += part

    @pl.when(step == pl.num_programs(0) - 1)
    def _():
        out_ref[...] = total_ref[...].astype(out_ref.dtype)


def project(tokens, factors, where, first, block, dtype):
    rows, width = tokens.shape
    rank = factors.shape[1]
    capacity = where.shape[0]
    offset = first // block

    def pick(slot):
        return pl.BlockSpec((1, rank, block), lambda k, where_ref: (where_ref[slot], 0, k + offset))

    return pl.pallas_call(
        functools.partial(proj_kernel, capacity),
        grid_spec=pltpu.PrefetchScalarGridSpec(
            num_scalar_prefetch=1,
            grid=(width // block,),
            in_specs=[pl.BlockSpec((rows, block), lambda k, where_ref: (0, k))]
            + [pick(slot) for slot in range(capacity)],
            out_specs=pl.BlockSpec((capacity * rank, rows), lambda k, where_ref: (0, 0)),
            scratch_shapes=[pltpu.VMEM((capacity * rank, rows), jnp.float32)],
        ),
        out_shape=jax.ShapeDtypeStruct((capacity * rank, rows), dtype),
        compiler_params=pltpu.CompilerParams(vmem_limit_bytes=32 << 20),
        cost_estimate=pl.CostEstimate(
            flops=2 * capacity * rank * rows * width,
            bytes_accessed=2 * width * (rows + capacity * rank),
            transcendentals=0,
        ),
        name="project",
    )(where, tokens, *([factors] * capacity))


def score_kernel(parts, hits_ref, live_ref, *refs):
    up_refs, down_refs, out_ref = refs[:parts], refs[parts : 2 * parts], refs[2 * parts]
    capacity = hits_ref.shape[1]
    rank = up_refs[0].shape[0] // capacity
    up = sum(ref[...].astype(jnp.float32) for ref in up_refs)
    down = sum(ref[...].astype(jnp.float32) for ref in down_refs)
    products = up * down
    dense = jnp.zeros((hits_ref.shape[0], products.shape[1]), jnp.float32)
    for slot in range(capacity):
        row = jnp.sum(products[slot * rank : (slot + 1) * rank], axis=0, keepdims=True)
        dense = dense + hits_ref[:, slot : slot + 1] * row
    out_ref[...] = (dense * live_ref[...]).T


def scores_of(hits, live, up_parts, down_parts):
    return pl.pallas_call(
        functools.partial(score_kernel, len(up_parts)),
        out_shape=jax.ShapeDtypeStruct((live.shape[1], hits.shape[0]), jnp.float32),
        name="scores",
    )(hits, live, *up_parts, *down_parts)


def spread(pieces_of, axis):
    return [
        pieces_of(0),
        shifted(pieces_of(1), **{axis: 1}),
        shifted(pieces_of(-1), **{axis: -1}),
        shifted(pieces_of(2), **{axis: 2}),
    ]


def gathered(block, axis):
    half = block.shape[0] // 2
    before = shifted(block, **{axis: 1})
    after = shifted(block, **{axis: -1})
    far_first = shifted(before[:half], **{axis: 1})
    far_second = shifted(after[half:], **{axis: -1})
    return jnp.concatenate([block, before, after, far_first, far_second], axis=0)


def body(
    hidden_acts,
    layer_inputs,
    norm_gains,
    top_cotangent,
    up_factors,
    down_factors,
    candidates,
    counts,
):
    sections = lax.axis_size("section")
    section = lax.axis_index("section")
    me = lax.axis_index("dp")
    shards = lax.axis_size("dp")
    c = me % CORES
    z = (me // CORES) % SIDE
    y = me // (CORES * SIDE)
    rows, width = layer_inputs.shape[1:]
    hidden = hidden_acts[0]
    up, down = up_factors[0, 0], down_factors[0, 0]
    ff = hidden.shape[1]
    rank = up.shape[0]
    up_wide, down_wide = ff // (2 * SIDE), width // (2 * SIDE)

    def columns(array, half, place, wide):
        start = half * SIDE * wide + (place % SIDE) * wide
        return lax.dynamic_slice_in_dim(array, start, wide, axis=1)

    queries, listed = candidates.shape
    capacity = listed + listed // 4
    member = jnp.any(
        candidates[:, :, None] == jnp.arange(shards, dtype=jnp.int32)[None, None, :], axis=1
    ).astype(jnp.int32)
    position = jnp.cumsum(member, axis=0) - member
    hits = (
        (member.T[:, None, :] == 1)
        & (position.T[:, None, :] == jnp.arange(capacity, dtype=jnp.int32)[None, :, None])
    )
    query = jnp.arange(queries, dtype=jnp.int32)
    order = jnp.array([0, 2, 3, 1], jnp.int32)
    far_y = order[(query // (CORES * SIDE) - y) % SIDE]
    far_z = order[(query // CORES % SIDE - z) % SIDE]
    other = (query % CORES != c).astype(jnp.int32) * SIDE * SIDE
    kept = (other + far_y * SIDE + far_z, other + far_z * SIDE + far_y)
    where = [jnp.sum(jnp.where(hits, place[None, None, :], 0), axis=2) for place in kept]
    own_hits = lax.dynamic_index_in_dim(hits, me, 0, keepdims=False).astype(jnp.float32).T
    live = (jnp.arange(rows, dtype=jnp.int32) < counts[0]).astype(jnp.float32)[None, :]

    places, axes, gather_axes = (z, y), ("dz", "dy"), ("dy", "dz")

    block = rows // sections
    inputs = lax.all_to_all(
        layer_inputs[0].reshape(sections, block, width), "section", 0, 0, tiled=True
    )
    gains = lax.all_gather(norm_gains, "section", axis=0, tiled=True)
    top = lax.dynamic_slice_in_dim(top_cotangent, section * block, block, axis=0)
    cotangents = chain(inputs, gains, top)
    cotangent = lax.all_to_all(cotangents, "section", 0, 0, tiled=True).reshape(rows, width)

    factors = []
    for half in range(2):
        pieces = spread(
            lambda d, half=half: jnp.concatenate(
                [
                    columns(up, half, places[half] + d, up_wide),
                    columns(down, half, places[half] + d, down_wide),
                ],
                axis=1,
            ),
            axes[half],
        )
        mine = gathered(jnp.concatenate(pieces, axis=0), gather_axes[half])
        whole = jnp.concatenate([mine, shifted(mine, dc=1)], axis=0)
        factors.append(whole.reshape(queries, rank, up_wide + down_wide))

    def shard_at(half, distance):
        if half == 0:
            return (y * SIDE + (z + distance) % SIDE) * CORES + c
        return (((y + distance) % SIDE) * SIDE + z) * CORES + c

    def partials(array, wide, first, block):
        parts = []
        for half in range(2):
            arrived = spread(
                lambda d, half=half: columns(array, half, places[half] + d, wide), axes[half]
            )
            for tokens, distance in zip(arrived, RELATIVE):
                listed_here = lax.dynamic_index_in_dim(
                    where[half], shard_at(half, distance), 0, keepdims=False
                )
                dtype = jnp.float32 if distance == 0 else jnp.bfloat16
                part = project(tokens, factors[half], listed_here, first, block, dtype)
                if distance:
                    part = shifted(part, **{axes[half]: distance})
                parts.append(part)
        return parts

    up_parts = partials(hidden, up_wide, 0, up_wide // 2)
    down_parts = partials(cotangent, down_wide, up_wide, down_wide // 2)
    return scores_of(own_hits, live, up_parts, down_parts)[None]


def solution(mesh):
    return jax.shard_map(
        body,
        mesh=mesh,
        in_specs=(
            P("section", "dp", None),
            P("section", "dp", None),
            P("section", None),
            P("dp", None),
            P("dp", "section", None, None),
            P("dp", "section", None, None),
            P(),
            P("dp"),
        ),
        out_specs=P("section", "dp", None),
        check_vma=False,
    )
```

```python
import functools

import jax
import jax.numpy as jnp
from jax import lax
from jax.experimental import pallas as pl
from jax.experimental.pallas import tpu as pltpu
from jax.sharding import Mesh
from jax.sharding import PartitionSpec as P

EPSILON = 1e-05
SIDE = 4
CORES = 2
RELATIVE = (0, 3, 1, 2)
HBM = pl.BlockSpec(memory_space=pltpu.HBM)
SMEM = pl.BlockSpec(memory_space=pltpu.SMEM)
TOKEN = jax.ShapeDtypeStruct((8, 128), jnp.float32)
VMEM_BYTES = 48 << 20


def shifted(block, axis, distance):
    size = lax.axis_size(axis)
    return lax.ppermute(block, axis, [(i, (i + distance) % size) for i in range(size)])


def moved(copies):
    for into, _ in copies:
        for copy in into:
            copy.start()
    for into, out in copies:
        for copy in into:
            copy.wait()
        out.start()
    for _, out in copies:
        out.wait()


def joined_kernel(groups, arrays, *refs):
    sources, held, sems = refs[:arrays], refs[-2], refs[-1]
    outs = refs[-3 - len(groups) : -3]
    copies, row = [], 0
    for group, out_ref in zip(groups, outs):
        to = 0
        for source, first, rows in group:
            here, i = held.at[pl.ds(row + to, rows)], len(copies)
            into = pltpu.make_async_copy(sources[source].at[pl.ds(first, rows)], here, sems.at[0, i])
            out = pltpu.make_async_copy(here, out_ref.at[pl.ds(to, rows)], sems.at[1, i])
            copies.append(([into], out))
            to += rows
        row += to
    moved(copies)


def joined(groups, after):
    arrays = []
    listed = []
    for group in groups:
        for array, _, _ in group:
            if not any(array is known for known in arrays):
                arrays.append(array)
        index = lambda array: [array is known for known in arrays].index(True)
        listed.append([(index(array), first, rows) for array, first, rows in group])
    sizes = [sum(rows for _, _, rows in group) for group in listed]
    wide, dtype = arrays[0].shape[1], arrays[0].dtype
    *outs, token = pl.pallas_call(
        functools.partial(joined_kernel, listed, len(arrays)),
        in_specs=[HBM] * (len(arrays) + len(after)),
        out_specs=[HBM] * (len(sizes) + 1),
        out_shape=[jax.ShapeDtypeStruct((size, wide), dtype) for size in sizes] + [TOKEN],
        scratch_shapes=[
            pltpu.VMEM((sum(sizes), wide), dtype),
            pltpu.SemaphoreType.DMA((2, sum(len(group) for group in listed))),
        ],
        compiler_params=pltpu.CompilerParams(vmem_limit_bytes=VMEM_BYTES),
        name="joined",
    )(*arrays, *after)
    return outs, token


def cut_kernel(wides, halves, steps, place_ref, *refs):
    arrays = refs[: len(wides)]
    held, sems = refs[-2:]
    outs = refs[-3 - halves * len(steps) : -3]
    copies = []
    for half in range(halves):
        for i, step in enumerate(steps):
            at = half * len(steps) + i
            place = (place_ref[half] + step) % SIDE
            to, into = 0, []
            for array, (array_ref, wide) in enumerate(zip(arrays, wides)):
                start = pl.multiple_of((half * SIDE + place) * wide, 128)
                into.append(
                    pltpu.make_async_copy(
                        array_ref.at[:, pl.ds(start, wide)],
                        held.at[at, :, pl.ds(to, wide)],
                        sems.at[array, at],
                    )
                )
                to += wide
            out = pltpu.make_async_copy(held.at[at], outs[at], sems.at[len(wides), at])
            copies.append((into, out))
    moved(copies)


def cut(arrays, places, steps, after):
    halves = 2
    wides = tuple(array.shape[1] // (halves * SIDE) for array in arrays)
    rows, wide = arrays[0].shape[0], sum(wides)
    count = halves * len(steps)
    dtype = arrays[0].dtype
    *pieces, token = pl.pallas_call(
        functools.partial(cut_kernel, wides, halves, steps),
        in_specs=[SMEM] + [HBM] * (len(arrays) + len(after)),
        out_specs=[HBM] * (count + 1),
        out_shape=[jax.ShapeDtypeStruct((rows, wide), dtype)] * count + [TOKEN],
        scratch_shapes=[
            pltpu.VMEM((count, rows, wide), dtype),
            pltpu.SemaphoreType.DMA((len(arrays) + 1, count)),
        ],
        compiler_params=pltpu.CompilerParams(vmem_limit_bytes=VMEM_BYTES),
        name="cut",
    )(places, *arrays, *after)
    return pieces[: len(steps)], pieces[len(steps) :], token


def chain_kernel(section_ref, inputs_ref, top_ref, *refs):
    gain_refs, out_refs = refs[:SIDE], refs[-3:-1]
    sections = inputs_ref.shape[0]
    wide = out_refs[0].shape[-1]

    def give(layer, values):
        for half, out_ref in enumerate(out_refs):
            for place in range(SIDE):
                start = (half * SIDE + place) * wide
                out_ref[layer, place] = values[:, start : start + wide]

    cotangent = top_ref[...].astype(jnp.float32)
    give(sections - 1, top_ref[...])
    for layer in range(sections - 1, 0, -1):
        distance = lax.rem(layer - section_ref[0] + sections, sections)
        gain = gain_refs[0][...]
        for kept, far in enumerate(RELATIVE):
            gain = jnp.where(distance == far, gain_refs[kept][...], gain)
        values = inputs_ref[layer].astype(jnp.float32)
        inverse = lax.rsqrt(jnp.mean(values * values, axis=-1, keepdims=True) + EPSILON)
        normed = values * inverse
        scaled = gain.astype(jnp.float32) * cotangent
        pulled = jnp.mean(normed * scaled, axis=-1, keepdims=True)
        cotangent = cotangent + scaled * inverse - normed * inverse * pulled
        give(layer - 1, cotangent.astype(jnp.bfloat16))


def chain(section, inputs, top, gains, after):
    sections, rows, width = inputs.shape
    step = 16
    steps = rows // step
    wide = width // (2 * SIDE)
    out = jax.ShapeDtypeStruct((sections, SIDE, rows, wide), jnp.bfloat16)
    first, second, token = pl.pallas_call(
        chain_kernel,
        grid_spec=pltpu.PrefetchScalarGridSpec(
            num_scalar_prefetch=1,
            grid=(steps,),
            in_specs=[
                pl.BlockSpec((sections, step, width), lambda i, section_ref: (0, i, 0)),
                pl.BlockSpec((step, width), lambda i, section_ref: (section_ref[0] * steps + i, 0)),
            ]
            + [pl.BlockSpec((1, width), lambda i, section_ref: (0, 0))] * len(gains)
            + [HBM] * len(after),
            out_specs=[
                pl.BlockSpec((sections, SIDE, step, wide), lambda i, section_ref: (0, 0, i, 0))
            ]
            * 2
            + [HBM],
        ),
        out_shape=[out, out, TOKEN],
        compiler_params=pltpu.CompilerParams(vmem_limit_bytes=VMEM_BYTES),
        name="cotangent_chain",
    )(section, inputs, top, *gains, *after)
    return (first, second), token


def project_kernel(groups, up_wide, at_ref, where_ref, up_ref, down_ref, mine_ref, theirs_ref, *refs):
    out_ref, _, factor_ref, token_ref, sems = refs[-5:]
    capacity = where_ref.shape[0]
    rank = factor_ref.shape[0] // capacity
    held = mine_ref.shape[0] // rank
    blocks, rows, down_wide = down_ref.shape[0], down_ref.shape[2], down_ref.shape[3]

    def slot_copy(source, row, slot):
        return pltpu.make_async_copy(
            source.at[pl.ds(pl.multiple_of(row * rank, rank), rank)],
            factor_ref.at[pl.ds(slot * rank, rank)],
            sems.at[slot],
        )

    copies = [
        pltpu.make_async_copy(
            up_ref.at[:, pl.ds(pl.multiple_of(at_ref[0], 128), up_wide)],
            token_ref.at[:, pl.ds(0, up_wide)],
            sems.at[capacity],
        )
    ] + [
        pltpu.make_async_copy(
            down_ref.at[block, at_ref[1]],
            token_ref.at[pl.ds(block * rows, rows), pl.ds(up_wide, down_wide)],
            sems.at[capacity + 1 + block],
        )
        for block in range(blocks)
    ]
    for copy in copies:
        copy.start()
    for slot in range(capacity):
        row = where_ref[slot]

        @pl.when(row < held)
        def _(row=row, slot=slot):
            slot_copy(mine_ref, row, slot).start()

        @pl.when(row >= held)
        def _(row=row, slot=slot):
            slot_copy(theirs_ref, row - held, slot).start()

    for copy in copies:
        copy.wait()
    size = capacity * rank
    slots = capacity // groups
    for group in range(groups):
        for slot in range(group * slots, (group + 1) * slots):
            slot_copy(mine_ref, 0, slot).wait()
        first, last = group * slots * rank, (group + 1) * slots * rank
        for side, columns in enumerate((slice(0, up_wide), slice(up_wide, up_wide + down_wide))):
            part = lax.dot_general(
                factor_ref[first:last, columns],
                token_ref[:, columns],
                (((1,), (1,)), ((), ())),
                preferred_element_type=jnp.float32,
            )
            out_ref[side * size + first : side * size + last] = part.astype(out_ref.dtype)


def project(at, where, up_tokens, down_tokens, mine, theirs, rank, up_wide, dtype, after, groups=2):
    capacity = where.shape[0]
    rows = up_tokens.shape[0]
    wide = mine.shape[1]
    return pl.pallas_call(
        functools.partial(project_kernel, groups, up_wide),
        in_specs=[SMEM, SMEM] + [HBM] * (4 + len(after)),
        out_specs=[pl.BlockSpec(memory_space=pltpu.VMEM), HBM],
        out_shape=[jax.ShapeDtypeStruct((2 * capacity * rank, rows), dtype), TOKEN],
        scratch_shapes=[
            pltpu.VMEM((capacity * rank, wide), jnp.bfloat16),
            pltpu.VMEM((rows, wide), jnp.bfloat16),
            pltpu.SemaphoreType.DMA((capacity + 1 + down_tokens.shape[0],)),
        ],
        compiler_params=pltpu.CompilerParams(vmem_limit_bytes=VMEM_BYTES),
        name="project",
    )(at, where, up_tokens, down_tokens, mine, theirs, *after)


def score_kernel(hits_ref, live_ref, *refs):
    part_refs, out_ref = refs[:-1], refs[-1]
    capacity = hits_ref.shape[1]
    size = part_refs[0].shape[0] // 2
    rank = size // capacity
    total = sum(ref[...].astype(jnp.float32) for ref in part_refs)
    products = total[:size] * total[size:]
    dense = jnp.zeros((hits_ref.shape[0], products.shape[1]), jnp.float32)
    for slot in range(capacity):
        row = jnp.sum(products[slot * rank : (slot + 1) * rank], axis=0, keepdims=True)
        dense = dense + hits_ref[:, slot : slot + 1] * row
    out_ref[...] = dense * live_ref[...]


def scores_of(hits, live, parts):
    return pl.pallas_call(
        score_kernel,
        out_shape=jax.ShapeDtypeStruct((hits.shape[0], live.shape[1]), jnp.float32),
        name="scores",
    )(hits, live, *parts).T


def spread(pieces, axis):
    return [shifted(piece, axis, distance) for piece, distance in zip(pieces, (1, -1, 2))]


def body(
    hidden_acts,
    layer_inputs,
    norm_gains,
    top_cotangent,
    up_factors,
    down_factors,
    candidates,
    counts,
):
    sections = lax.axis_size("x")
    section, y, z, c = (lax.axis_index(axis) for axis in ("x", "y", "z", "c"))
    me = (y * SIDE + z) * CORES + c
    shards = SIDE * SIDE * CORES
    rows, width = layer_inputs.shape[1:]
    hidden = hidden_acts[0]
    up, down = up_factors[0, 0], down_factors[0, 0]
    rank, ff = up.shape
    up_wide = ff // (2 * SIDE)
    places = jnp.stack([z, y]).astype(jnp.int32)
    axes, other_axes = ("z", "y"), ("y", "z")
    halves = range(2)

    def whole(array):
        return (array, 0, array.shape[0])

    *pieces, token = cut([up, down], places, (0, 1, -1, 2), [])
    near, token = joined(
        [
            [whole(pieces[half][0])] + [whole(p) for p in spread(pieces[half][1:], axes[half])]
            for half in halves
        ],
        [token],
    )
    size = near[0].shape[0]
    before = [shifted(near[half], other_axes[half], 1) for half in halves]
    after = [shifted(near[half], other_axes[half], -1) for half in halves]
    *sent, token = cut([hidden], places, (1, -1, 2), [token])

    block = rows // sections
    gains = [norm_gains] + [shifted(norm_gains, "x", distance) for distance in (1, -1, 2)]
    inputs = lax.all_to_all(
        layer_inputs[0].reshape(sections, block, width), "x", 0, 0, tiled=True
    )
    cotangents, token = chain(
        section.reshape(1).astype(jnp.int32), inputs, top_cotangent, gains, [token]
    )
    down_tokens = [
        lax.all_to_all(
            cotangents[half].reshape(sections * SIDE, block, -1), ("x", axes[half]), 0, 0, tiled=True
        ).reshape(sections, SIDE, block, -1)
        for half in halves
    ]

    forward, token = joined(
        [[(array, half * size // 2, size // 2)] for half in halves for array in (before, after)[half]],
        [token],
    )
    far = [
        (shifted(forward[half], other_axes[half], 1), shifted(forward[2 + half], other_axes[half], -1))
        for half in halves
    ]
    arrived = [spread(sent[half], axes[half]) for half in halves]
    mine, token = joined(
        [
            [whole(near[half]), whole(before[half]), whole(after[half])]
            + [whole(part) for part in far[half]]
            for half in halves
        ],
        [token, arrived[0][2], down_tokens[0]],
    )
    theirs = [shifted(mine[half], "c", 1) for half in halves]

    queries, listed = candidates.shape
    capacity = listed + listed // 4
    member = jnp.any(
        candidates[:, :, None] == jnp.arange(shards, dtype=jnp.int32)[None, None, :], axis=1
    ).astype(jnp.int32)
    position = jnp.cumsum(member, axis=0) - member
    hits = (
        (member.T[:, None, :] == 1)
        & (position.T[:, None, :] == jnp.arange(capacity, dtype=jnp.int32)[None, :, None])
    )
    query = jnp.arange(queries, dtype=jnp.int32)
    order = jnp.array([0, 2, 3, 1], jnp.int32)
    far_y = order[(query // (CORES * SIDE) - y) % SIDE]
    far_z = order[(query // CORES % SIDE - z) % SIDE]
    other = (query % CORES != c).astype(jnp.int32) * SIDE * SIDE
    kept = (other + far_y * SIDE + far_z, other + far_z * SIDE + far_y)
    where = [jnp.sum(jnp.where(hits, place[None, None, :], 0), axis=2) for place in kept]
    own_hits = lax.dynamic_index_in_dim(hits, me, 0, keepdims=False).astype(jnp.float32).T
    live = (jnp.arange(rows, dtype=jnp.int32) < counts[0]).astype(jnp.float32)[None, :]

    parts = []
    for kept_at in range(SIDE):
        for half in halves:
            distance = RELATIVE[kept_at]
            place = (places[half] + distance) % SIDE
            shard = (
                (y * SIDE + place) * CORES + c if half == 0 else (place * SIDE + z) * CORES + c
            )
            column = jnp.int32(0) if distance else (half * SIDE + place) * up_wide
            part, token = project(
                jnp.stack([column, place]).astype(jnp.int32),
                lax.dynamic_index_in_dim(where[half], shard, 0, keepdims=False),
                arrived[half][kept_at - 1] if distance else hidden,
                down_tokens[half],
                mine[half],
                theirs[half],
                rank,
                up_wide,
                jnp.bfloat16 if distance else jnp.float32,
                [token],
            )
            parts.append(shifted(part, axes[half], distance) if distance else part)
    return scores_of(own_hits, live, parts)[None]


def solution(mesh):
    grid = Mesh(mesh.devices.reshape(-1, SIDE, SIDE, CORES), ("x", "y", "z", "c"))
    dp = ("y", "z", "c")
    return jax.shard_map(
        body,
        mesh=grid,
        in_specs=(
            P("x", dp, None),
            P("x", dp, None),
            P("x", None),
            P(dp, None),
            P(dp, "x", None, None),
            P(dp, "x", None, None),
            P(),
            P(dp),
        ),
        out_specs=P("x", dp, None),
        check_vma=False,
    )
```

```python
import functools

import jax
import jax.numpy as jnp
from jax import lax
from jax.experimental import pallas as pl
from jax.experimental.pallas import tpu as pltpu
from jax.sharding import Mesh
from jax.sharding import PartitionSpec as P

EPSILON = 1e-05
SIDE = 4
CORES = 2
RELATIVE = (0, 3, 1, 2)
ANY = pl.BlockSpec(memory_space=pl.ANY)
SMEM = pl.BlockSpec(memory_space=pltpu.SMEM)
TOKEN = jax.ShapeDtypeStruct((8, 128), jnp.float32)
VMEM_BYTES = 60 << 20


def shifted(block, axis, distance):
    size = lax.axis_size(axis)
    return lax.ppermute(block, axis, [(i, (i + distance) % size) for i in range(size)])


def moved(copies):
    for into, _ in copies:
        for copy in into:
            copy.start()
    for into, out in copies:
        for copy in into:
            copy.wait()
        out.start()
    for _, out in copies:
        out.wait()


def joined_kernel(groups, arrays, *refs):
    sources, held, sems = refs[:arrays], refs[-2], refs[-1]
    outs = refs[-3 - len(groups) : -3]
    copies, row = [], 0
    for group, out_ref in zip(groups, outs):
        to = 0
        for source, first, rows in group:
            here, i = held.at[pl.ds(row + to, rows)], len(copies)
            into = pltpu.make_async_copy(sources[source].at[pl.ds(first, rows)], here, sems.at[0, i])
            out = pltpu.make_async_copy(here, out_ref.at[pl.ds(to, rows)], sems.at[1, i])
            copies.append(([into], out))
            to += rows
        row += to
    moved(copies)


def joined(groups, after):
    arrays = []
    listed = []
    for group in groups:
        for array, _, _ in group:
            if not any(array is known for known in arrays):
                arrays.append(array)
        index = lambda array: [array is known for known in arrays].index(True)
        listed.append([(index(array), first, rows) for array, first, rows in group])
    sizes = [sum(rows for _, _, rows in group) for group in listed]
    wide, dtype = arrays[0].shape[1], arrays[0].dtype
    *outs, token = pl.pallas_call(
        functools.partial(joined_kernel, listed, len(arrays)),
        in_specs=[ANY] * (len(arrays) + len(after)),
        out_specs=[ANY] * (len(sizes) + 1),
        out_shape=[jax.ShapeDtypeStruct((size, wide), dtype) for size in sizes] + [TOKEN],
        scratch_shapes=[
            pltpu.VMEM((sum(sizes), wide), dtype),
            pltpu.SemaphoreType.DMA((2, sum(len(group) for group in listed))),
        ],
        compiler_params=pltpu.CompilerParams(vmem_limit_bytes=VMEM_BYTES),
        name="joined",
    )(*arrays, *after)
    return outs, token


def cut_kernel(plan, arrays, *refs):
    sources = refs[:arrays]
    count = len(plan)
    outs, held, sems = refs[-2 - 2 * count : -2 - count], refs[-1 - count : -1], refs[-1]
    copies = []
    for at, (sources_of, out_ref, buffer) in enumerate(zip(plan, outs, held)):
        into = []
        for source, rows, to_row, to, first, wide, by, step in sources_of:
            start = first
            if by is not None:
                start = pl.multiple_of(first + (lax.axis_index(by) + step) % SIDE * wide, 128)
            into.append(
                pltpu.make_async_copy(
                    sources[source].at[pl.ds(*rows), pl.ds(start, wide)],
                    buffer.at[pl.ds(to_row, rows[1]), pl.ds(to, wide)],
                    sems.at[at, len(into)],
                )
            )
        copies.append((into, pltpu.make_async_copy(buffer, out_ref, sems.at[at, len(into)])))
    moved(copies)


def cut(arrays, plan, after):
    shapes = [
        (max(to_row + rows[1] for _, rows, to_row, *_ in item), max(to + wide for _, _, _, to, _, wide, *_ in item))
        for item in plan
    ]
    dtype = arrays[0].dtype
    *outs, token = pl.pallas_call(
        functools.partial(cut_kernel, plan, len(arrays)),
        in_specs=[ANY] * (len(arrays) + len(after)),
        out_specs=[ANY] * (len(plan) + 1),
        out_shape=[jax.ShapeDtypeStruct(shape, dtype) for shape in shapes] + [TOKEN],
        scratch_shapes=[pltpu.VMEM(shape, dtype) for shape in shapes]
        + [pltpu.SemaphoreType.DMA((len(plan), 1 + max(len(item) for item in plan)))],
        compiler_params=pltpu.CompilerParams(vmem_limit_bytes=VMEM_BYTES),
        name="cut",
    )(*arrays, *after)
    return outs, token


def chain_kernel(section_ref, inputs_ref, gains_ref, top_ref, *refs):
    out_ref = refs[-2]
    sections, width = inputs_ref.shape[0], top_ref.shape[1]
    cotangent = top_ref[...].astype(jnp.float32)
    out_ref[sections - 1] = top_ref[...]
    for layer in range(sections - 1, 0, -1):
        gain = gains_ref[layer : layer + 1, :].astype(jnp.float32)
        values = inputs_ref[layer, :, :width].astype(jnp.float32)
        inverse = lax.rsqrt(jnp.mean(values * values, axis=-1, keepdims=True) + EPSILON)
        normed = values * inverse
        scaled = gain * cotangent
        pulled = jnp.mean(normed * scaled, axis=-1, keepdims=True)
        cotangent = cotangent + scaled * inverse - normed * inverse * pulled
        out_ref[layer - 1] = cotangent.astype(out_ref.dtype)


def chain(section, inputs, gains, top, after):
    sections, rows, wide_in = inputs.shape
    width = top.shape[1]
    step = 16
    steps = rows // step
    return pl.pallas_call(
        chain_kernel,
        grid_spec=pltpu.PrefetchScalarGridSpec(
            num_scalar_prefetch=1,
            grid=(steps,),
            in_specs=[
                pl.BlockSpec((sections, step, wide_in), lambda i, section_ref: (0, i, 0)),
                pl.BlockSpec((sections, width), lambda i, section_ref: (0, 0)),
                pl.BlockSpec((step, width), lambda i, section_ref: (section_ref[0] * steps + i, 0)),
            ]
            + [ANY] * len(after),
            out_specs=[
                pl.BlockSpec((sections, step, width), lambda i, section_ref: (0, i, 0)),
                ANY,
            ],
        ),
        out_shape=[jax.ShapeDtypeStruct((sections, rows, width), jnp.bfloat16), TOKEN],
        compiler_params=pltpu.CompilerParams(vmem_limit_bytes=VMEM_BYTES),
        name="cotangent_chain",
    )(section, inputs, gains, top, *after)


def project_kernel(plan, sources, kept, up_wide, down_wide, where_ref, *refs):
    pieces = len(plan)
    factor_refs, token_refs = refs[:kept], refs[kept:]
    outs = refs[-4 - pieces : -4]
    factor_ref, token_ref, sems = refs[-3:]
    capacity = where_ref.shape[1]
    rank = factor_ref.shape[1] // capacity
    held = factor_refs[0].shape[0] // rank
    halves = 2
    y, z, c = (lax.axis_index(axis) for axis in ("y", "z", "c"))
    wides = up_wide, down_wide

    def place_of(piece):
        half, distance = plan[piece]
        return ((y if half else z) + distance) % SIDE

    def row_of(piece):
        half, _ = plan[piece]
        place = place_of(piece)
        shard = (place * SIDE + z) * CORES + c if half else (y * SIDE + place) * CORES + c
        return half * (where_ref.shape[0] // halves) + shard

    def slot_copy(source, row, piece, slot):
        return pltpu.make_async_copy(
            source.at[pl.ds(pl.multiple_of(row * rank, rank), rank)],
            factor_ref.at[piece, pl.ds(slot * rank, rank)],
            sems.at[piece, slot],
        )

    def token_copies(piece):
        to, copies = 0, []
        for part, wide in enumerate(wides):
            source, column = sources[piece][part]
            if column is None:
                column = pl.multiple_of((plan[piece][0] * SIDE + place_of(piece)) * wide, 128)
            copies.append(
                pltpu.make_async_copy(
                    token_refs[source].at[:, pl.ds(column, wide)],
                    token_ref.at[piece, :, pl.ds(to, wide)],
                    sems.at[piece, capacity + part],
                )
            )
            to += wide
        return copies

    def begin(piece):
        half, _ = plan[piece]
        for copy in token_copies(piece):
            copy.start()
        listed = row_of(piece)
        here = factor_refs[half * (kept // halves) : (half + 1) * (kept // halves)]
        for slot in range(capacity):
            row = where_ref[listed, slot]
            for at, source in enumerate(here):

                @pl.when((row >= at * held) & (row < (at + 1) * held))
                def _(source=source, row=row, at=at, slot=slot, piece=piece):
                    slot_copy(source, row - at * held, piece, slot).start()

    size = capacity * rank
    ahead = 2
    for piece in range(min(ahead, pieces)):
        begin(piece)
    for piece, out_ref in enumerate(outs):
        for copy in token_copies(piece):
            copy.wait()
        for slot in range(capacity):
            slot_copy(factor_refs[0], 0, piece, slot).wait()
        if piece + ahead < pieces:
            begin(piece + ahead)
        for side, columns in enumerate((slice(0, up_wide), slice(up_wide, up_wide + down_wide))):
            part = lax.dot_general(
                factor_ref[piece, :, columns],
                token_ref[piece, :, columns],
                (((1,), (1,)), ((), ())),
                preferred_element_type=jnp.float32,
            )
            out_ref[side * size : (side + 1) * size] = part.astype(out_ref.dtype)


def project(plan, where, tokens, factors, rank, up_wide, down_wide, after):
    pieces, capacity = len(plan), where.shape[1]
    rows = tokens[0][0][0].shape[0]
    arrays = []
    sources = []
    for pair in tokens:
        for array, _ in pair:
            if not any(array is known for known in arrays):
                arrays.append(array)
        sources.append(
            [([array is known for known in arrays].index(True), column) for array, column in pair]
        )
    vmem = pl.BlockSpec(memory_space=pltpu.VMEM)
    *outs, token = pl.pallas_call(
        functools.partial(project_kernel, plan, sources, len(factors), up_wide, down_wide),
        in_specs=[SMEM] + [ANY] * (len(factors) + len(arrays) + len(after)),
        out_specs=[vmem] * pieces + [ANY],
        out_shape=[
            jax.ShapeDtypeStruct(
                (2 * capacity * rank, rows), jnp.bfloat16 if distance else jnp.float32
            )
            for _, distance in plan
        ]
        + [TOKEN],
        scratch_shapes=[
            pltpu.VMEM((pieces, capacity * rank, up_wide + down_wide), jnp.bfloat16),
            pltpu.VMEM((pieces, rows, up_wide + down_wide), jnp.bfloat16),
            pltpu.SemaphoreType.DMA((pieces, capacity + 2)),
        ],
        compiler_params=pltpu.CompilerParams(vmem_limit_bytes=VMEM_BYTES),
        name="project",
    )(where, *factors, *arrays, *after)
    return outs, token


def score_kernel(hits_ref, live_ref, *refs):
    part_refs, out_ref = refs[:-1], refs[-1]
    capacity = hits_ref.shape[1]
    size = part_refs[0].shape[0] // 2
    rank = size // capacity
    total = sum(ref[...].astype(jnp.float32) for ref in part_refs)
    products = total[:size] * total[size:]
    dense = jnp.zeros((hits_ref.shape[0], products.shape[1]), jnp.float32)
    for slot in range(capacity):
        row = jnp.sum(products[slot * rank : (slot + 1) * rank], axis=0, keepdims=True)
        dense = dense + hits_ref[:, slot : slot + 1] * row
    out_ref[...] = dense * live_ref[...]


def scores_of(hits, live, parts):
    return pl.pallas_call(
        score_kernel,
        out_shape=jax.ShapeDtypeStruct((hits.shape[0], live.shape[1]), jnp.float32),
        name="scores",
    )(hits, live, *parts).T


def spread(pieces, axis):
    return [shifted(piece, axis, distance) for piece, distance in zip(pieces, (1, -1, 2))]


def body(
    hidden_acts,
    layer_inputs,
    norm_gains,
    top_cotangent,
    up_factors,
    down_factors,
    candidates,
    counts,
):
    sections = lax.axis_size("x")
    section, y, z, c = (lax.axis_index(axis) for axis in ("x", "y", "z", "c"))
    me = (y * SIDE + z) * CORES + c
    shards = SIDE * SIDE * CORES
    rows, width = layer_inputs.shape[1:]
    hidden = hidden_acts[0]
    up, down = up_factors[0, 0], down_factors[0, 0]
    rank, ff = up.shape
    up_wide = ff // (2 * SIDE)
    down_wide = width // (2 * SIDE)
    axes, other_axes = ("z", "y"), ("y", "z")
    halves = range(2)

    def whole(array):
        return (array, 0, array.shape[0])

    def slices(half, sources, wides, rows, steps):
        items = []
        for step in steps:
            to, item = 0, []
            for source, wide in zip(sources, wides):
                item.append((source, (0, rows), 0, to, half * SIDE * wide, wide, axes[half], step))
                to += wide
            items.append(item)
        return items

    queries, listed = candidates.shape
    capacity = listed + listed // 4
    member = jnp.any(
        candidates[:, :, None] == jnp.arange(shards, dtype=jnp.int32)[None, None, :], axis=1
    ).astype(jnp.int32)
    position = jnp.cumsum(member, axis=0) - member
    hits = (
        (member.T[:, None, :] == 1)
        & (position.T[:, None, :] == jnp.arange(capacity, dtype=jnp.int32)[None, :, None])
    )
    query = jnp.arange(queries, dtype=jnp.int32)
    order = jnp.array([0, 2, 3, 1], jnp.int32)
    far_y = order[(query // (CORES * SIDE) - y) % SIDE]
    far_z = order[(query // CORES % SIDE - z) % SIDE]
    other = (query % CORES != c).astype(jnp.int32) * SIDE * SIDE
    kept = (other + far_y * SIDE + far_z, other + far_z * SIDE + far_y)
    where = jnp.concatenate(
        [jnp.sum(jnp.where(hits, place[None, None, :], 0), axis=2) for place in kept]
    )
    own_hits = lax.dynamic_index_in_dim(hits, me, 0, keepdims=False).astype(jnp.float32).T
    live = (jnp.arange(rows, dtype=jnp.int32) < counts[0]).astype(jnp.float32)[None, :]

    outs, token = cut(
        [up, down, hidden],
        [item for half in halves for item in slices(half, (2,), (up_wide,), rows, (2,))]
        + [
            item
            for half in halves
            for item in slices(half, (0, 1), (up_wide, down_wide), rank, (0, 1, -1, 2))
        ],
        [],
    )
    far_up = [shifted(outs[half], axes[half], 2) for half in halves]
    pieces = outs[2 : 2 + SIDE], outs[2 + SIDE :]
    block = rows // sections
    extra = width // block
    (payload,), token = cut(
        [layer_inputs[0], norm_gains.reshape(block, extra)],
        [
            [
                item
                for part in range(sections)
                for item in (
                    (0, (part * block, block), part * block, 0, 0, width, None, 0),
                    (1, (0, block), part * block, width, 0, extra, None, 0),
                )
            ]
        ],
        [token],
    )
    inputs = lax.all_to_all(payload.reshape(sections, block, -1), "x", 0, 0, tiled=True)
    gains = inputs[:, :, width:].reshape(sections, width)

    near, token = joined(
        [
            [whole(pieces[half][0])] + [whole(p) for p in spread(pieces[half][1:], axes[half])]
            for half in halves
        ],
        [token],
    )
    size = near[0].shape[0]
    before = [shifted(near[half], other_axes[half], 1) for half in halves]
    after = [shifted(near[half], other_axes[half], -1) for half in halves]

    cotangents, token = chain(
        section.reshape(1).astype(jnp.int32),
        inputs,
        gains,
        top_cotangent,
        [token, where, own_hits, live],
    )
    cotangent = lax.all_to_all(cotangents, "x", 0, 0, tiled=True).reshape(rows, width)

    forward, token = joined(
        [[(array, half * size // 2, size // 2)] for half in halves for array in (before, after)[half]],
        [token],
    )
    far = [
        (shifted(forward[half], other_axes[half], 1), shifted(forward[2 + half], other_axes[half], -1))
        for half in halves
    ]
    sent, token = cut(
        [hidden, cotangent],
        [item for half in halves for item in slices(half, (1,), (down_wide,), rows, (2,))]
        + [
            item
            for half in halves
            for item in slices(half, (0, 1), (up_wide, down_wide), rows, (1, -1))
        ],
        [token],
    )
    far_down = [shifted(sent[half], axes[half], 2) for half in halves]
    beside = [
        [shifted(sent[2 + 2 * half], axes[half], 1), shifted(sent[3 + 2 * half], axes[half], -1)]
        for half in halves
    ]
    mine, token = joined(
        [
            [whole(part) for part in (near[half], before[half], after[half], *far[half])]
            for half in halves
        ],
        [token],
    )
    factors = [array for half in halves for array in (mine[half], shifted(mine[half], "c", 1))]

    parts = []
    for distances in ((0, 2), (3, 1)):
        plan = [(half, distance) for half in halves for distance in distances]
        tokens = []
        for half, distance in plan:
            if distance == 0:
                tokens.append(((hidden, None), (cotangent, None)))
            elif distance == 2:
                tokens.append(((far_up[half], 0), (far_down[half], 0)))
            else:
                piece = beside[half][RELATIVE.index(distance) - 1]
                tokens.append(((piece, 0), (piece, up_wide)))
        products, token = project(plan, where, tokens, factors, rank, up_wide, down_wide, [token])
        parts += [
            shifted(product, axes[half], distance) if distance else product
            for product, (half, distance) in zip(products, plan)
        ]
    return scores_of(own_hits, live, parts)[None]


def solution(mesh):
    grid = Mesh(mesh.devices.reshape(-1, SIDE, SIDE, CORES), ("x", "y", "z", "c"))
    dp = ("y", "z", "c")
    return jax.shard_map(
        body,
        mesh=grid,
        in_specs=(
            P("x", dp, None),
            P("x", dp, None),
            P("x", None),
            P(dp, None),
            P(dp, "x", None, None),
            P(dp, "x", None, None),
            P(),
            P(dp),
        ),
        out_specs=P("x", dp, None),
        check_vma=False,
    )
```

```python
import functools

import jax
import jax.numpy as jnp
from jax import lax
from jax.experimental import pallas as pl
from jax.experimental.pallas import tpu as pltpu
from jax.sharding import Mesh
from jax.sharding import PartitionSpec as P

EPSILON = 1e-05
SIDE = 4
CORES = 2
RELATIVE = (0, 3, 1, 2)
ANY = pl.BlockSpec(memory_space=pl.ANY)
SMEM = pl.BlockSpec(memory_space=pltpu.SMEM)
TOKEN = jax.ShapeDtypeStruct((8, 128), jnp.float32)
VMEM_BYTES = 60 << 20


def shifted(block, axis, distance):
    size = lax.axis_size(axis)
    return lax.ppermute(block, axis, [(i, (i + distance) % size) for i in range(size)])


def moved(copies):
    for into, _ in copies:
        for copy in into:
            copy.start()
    for into, out in copies:
        for copy in into:
            copy.wait()
        out.start()
    for _, out in copies:
        out.wait()


def joined_kernel(blocks, arrays, *refs):
    sources, held, sems = refs[:arrays], refs[-2], refs[-1]
    outs = refs[-4 - max(out for out, *_ in blocks) : -3]
    copies, row = [], 0
    for i, (out, to, source, first, rows) in enumerate(blocks):
        here = held.at[pl.ds(row, rows)]
        into = pltpu.make_async_copy(sources[source].at[pl.ds(first, rows)], here, sems.at[0, i])
        copies.append(
            ([into], pltpu.make_async_copy(here, outs[out].at[pl.ds(to, rows)], sems.at[1, i]))
        )
        row += rows
    moved(copies)


def joined(groups, after, into=None):
    arrays, blocks = [], []
    for out, (_, *group) in enumerate(groups):
        for to, array, first, rows in group:
            if not any(array is known for known in arrays):
                arrays.append(array)
            source = [array is known for known in arrays].index(True)
            blocks.append((out, to, source, first, rows))
    wide, dtype = arrays[0].shape[1], arrays[0].dtype
    into = [] if into is None else [into]
    *outs, token = pl.pallas_call(
        functools.partial(joined_kernel, blocks, len(arrays)),
        in_specs=[ANY] * (len(arrays) + len(into) + len(after)),
        out_specs=[ANY] * (len(groups) + 1),
        out_shape=[jax.ShapeDtypeStruct((size, wide), dtype) for size, *_ in groups] + [TOKEN],
        scratch_shapes=[
            pltpu.VMEM((sum(block[-1] for block in blocks), wide), dtype),
            pltpu.SemaphoreType.DMA((2, len(blocks))),
        ],
        input_output_aliases={len(arrays) + i: i for i in range(len(into))},
        compiler_params=pltpu.CompilerParams(vmem_limit_bytes=VMEM_BYTES),
        name="joined",
    )(*arrays, *into, *after)
    return outs, token


def cut_kernel(plan, arrays, starts, *refs):
    sources = refs[:arrays]
    count = len(plan)
    outs, held, sems = refs[-2 - 2 * count : -2 - count], refs[-1 - count : -1], refs[-1]
    copies = []
    for at, (sources_of, out_ref, buffer) in enumerate(zip(plan, outs, held)):
        into = []
        for source, rows, to_row, to, first, wide, by, step in sources_of:
            start = first
            if by is not None:
                start = pl.multiple_of(first + (lax.axis_index(by) + step) % SIDE * wide, 128)
            into.append(
                pltpu.make_async_copy(
                    sources[source].at[pl.ds(*rows), pl.ds(start, wide)],
                    buffer.at[pl.ds(to_row, rows[1]), pl.ds(to, wide)],
                    sems.at[at, len(into)],
                )
            )
        target = out_ref.at[:, pl.ds(starts[at], buffer.shape[1])]
        copies.append((into, pltpu.make_async_copy(buffer, target, sems.at[at, len(into)])))
    moved(copies)


def cut(arrays, plan, after, wide=None, into=None, start=0):
    shapes = [
        (max(to_row + rows[1] for _, rows, to_row, *_ in item), max(to + columns for _, _, _, to, _, columns, *_ in item))
        for item in plan
    ]
    dtype = arrays[0].dtype
    into = into or []
    *outs, token = pl.pallas_call(
        functools.partial(cut_kernel, plan, len(arrays), [start] * len(plan)),
        in_specs=[ANY] * (len(arrays) + len(into) + len(after)),
        out_specs=[ANY] * (len(plan) + 1),
        out_shape=[jax.ShapeDtypeStruct((shape[0], wide or shape[1]), dtype) for shape in shapes]
        + [TOKEN],
        scratch_shapes=[pltpu.VMEM(shape, dtype) for shape in shapes]
        + [pltpu.SemaphoreType.DMA((len(plan), 1 + max(len(item) for item in plan)))],
        input_output_aliases={len(arrays) + i: i for i in range(len(into))},
        compiler_params=pltpu.CompilerParams(vmem_limit_bytes=VMEM_BYTES),
        name="cut",
    )(*arrays, *into, *after)
    return outs, token


def chain_kernel(section_ref, inputs_ref, gains_ref, top_ref, *refs):
    out_ref = refs[-2]
    sections, width = inputs_ref.shape[0], top_ref.shape[1]
    cotangent = top_ref[...].astype(jnp.float32)
    out_ref[sections - 1] = top_ref[...]
    for layer in range(sections - 1, 0, -1):
        gain = gains_ref[layer : layer + 1, :].astype(jnp.float32)
        values = inputs_ref[layer, :, :width].astype(jnp.float32)
        inverse = lax.rsqrt(jnp.mean(values * values, axis=-1, keepdims=True) + EPSILON)
        normed = values * inverse
        scaled = gain * cotangent
        pulled = jnp.mean(normed * scaled, axis=-1, keepdims=True)
        cotangent = cotangent + scaled * inverse - normed * inverse * pulled
        out_ref[layer - 1] = cotangent.astype(out_ref.dtype)


def chain(section, inputs, gains, top, after):
    sections, rows, wide_in = inputs.shape
    width = top.shape[1]
    step = 16
    steps = rows // step
    return pl.pallas_call(
        chain_kernel,
        grid_spec=pltpu.PrefetchScalarGridSpec(
            num_scalar_prefetch=1,
            grid=(steps,),
            in_specs=[
                pl.BlockSpec((sections, step, wide_in), lambda i, section_ref: (0, i, 0)),
                pl.BlockSpec((sections, width), lambda i, section_ref: (0, 0)),
                pl.BlockSpec((step, width), lambda i, section_ref: (section_ref[0] * steps + i, 0)),
            ]
            + [ANY] * len(after),
            out_specs=[
                pl.BlockSpec((sections, step, width), lambda i, section_ref: (0, i, 0)),
                ANY,
            ],
        ),
        out_shape=[jax.ShapeDtypeStruct((sections, rows, width), jnp.bfloat16), TOKEN],
        compiler_params=pltpu.CompilerParams(vmem_limit_bytes=VMEM_BYTES),
        name="cotangent_chain",
    )(section, inputs, gains, top, *after)


def project_kernel(plan, sources, up_wide, down_wide, where_ref, *refs):
    pieces = len(plan)
    factor_refs, token_refs = refs[:CORES], refs[CORES:]
    outs = refs[-4 - pieces : -4]
    factor_ref, token_ref, sems = refs[-3:]
    capacity = where_ref.shape[1]
    rank = factor_ref.shape[1] // capacity
    halves = 2
    y, z, c = (lax.axis_index(axis) for axis in ("y", "z", "c"))
    wides = up_wide, down_wide

    def place_of(piece):
        half, distance = plan[piece]
        return ((y if half else z) + distance) % SIDE

    def row_of(piece):
        half, _ = plan[piece]
        place = place_of(piece)
        shard = (place * SIDE + z) * CORES + c if half else (y * SIDE + place) * CORES + c
        return half * (where_ref.shape[0] // halves) + shard

    def slot_copy(source, row, piece, slot):
        return pltpu.make_async_copy(
            source.at[pl.ds(pl.multiple_of(row * rank, rank), rank)],
            factor_ref.at[piece, pl.ds(slot * rank, rank)],
            sems.at[piece, slot],
        )

    def token_copies(piece):
        to, copies = 0, []
        for part, wide in enumerate(wides):
            source, column = sources[piece][part]
            if column is None:
                column = pl.multiple_of((plan[piece][0] * SIDE + place_of(piece)) * wide, 128)
            copies.append(
                pltpu.make_async_copy(
                    token_refs[source].at[:, pl.ds(column, wide)],
                    token_ref.at[piece, :, pl.ds(to, wide)],
                    sems.at[piece, capacity + part],
                )
            )
            to += wide
        return copies

    groups = 2
    slots = capacity // groups
    chunks = [(piece, group) for piece in range(pieces) for group in range(groups)]

    def begin(piece, group):
        half, _ = plan[piece]
        if group == 0:
            for copy in token_copies(piece):
                copy.start()
        listed = row_of(piece)
        held = SIDE * SIDE
        for slot in range(group * slots, (group + 1) * slots):
            row = where_ref[listed, slot]
            for core, source in enumerate(factor_refs):

                @pl.when(row // held == core)
                def _(source=source, row=half * held + row % held, slot=slot, piece=piece):
                    slot_copy(source, row, piece, slot).start()

    size = capacity * rank
    ahead = 2
    for chunk in chunks[:ahead]:
        begin(*chunk)
    for at, (piece, group) in enumerate(chunks):
        if group == 0:
            for copy in token_copies(piece):
                copy.wait()
        for slot in range(group * slots, (group + 1) * slots):
            slot_copy(factor_refs[0], 0, piece, slot).wait()
        if at + ahead < len(chunks):
            begin(*chunks[at + ahead])
        first, last = group * slots * rank, (group + 1) * slots * rank
        for side, columns in enumerate((slice(0, up_wide), slice(up_wide, up_wide + down_wide))):
            part = lax.dot_general(
                factor_ref[piece, first:last, columns],
                token_ref[piece, :, columns],
                (((1,), (1,)), ((), ())),
                preferred_element_type=jnp.float32,
            )
            outs[piece][side * size + first : side * size + last] = part.astype(outs[piece].dtype)


def project(plan, where, tokens, factors, rank, up_wide, down_wide, after):
    pieces, capacity = len(plan), where.shape[1]
    rows = tokens[0][0][0].shape[0]
    arrays = []
    sources = []
    for pair in tokens:
        for array, _ in pair:
            if not any(array is known for known in arrays):
                arrays.append(array)
        sources.append(
            [([array is known for known in arrays].index(True), column) for array, column in pair]
        )
    vmem = pl.BlockSpec(memory_space=pltpu.VMEM)
    *outs, token = pl.pallas_call(
        functools.partial(project_kernel, plan, sources, up_wide, down_wide),
        in_specs=[SMEM] + [ANY] * (len(factors) + len(arrays) + len(after)),
        out_specs=[vmem] * pieces + [ANY],
        out_shape=[
            jax.ShapeDtypeStruct(
                (2 * capacity * rank, rows), jnp.bfloat16 if distance else jnp.float32
            )
            for _, distance in plan
        ]
        + [TOKEN],
        scratch_shapes=[
            pltpu.VMEM((pieces, capacity * rank, up_wide + down_wide), jnp.bfloat16),
            pltpu.VMEM((pieces, rows, up_wide + down_wide), jnp.bfloat16),
            pltpu.SemaphoreType.DMA((pieces, capacity + 2)),
        ],
        compiler_params=pltpu.CompilerParams(vmem_limit_bytes=VMEM_BYTES),
        name="project",
    )(where, *factors, *arrays, *after)
    return outs, token


def score_kernel(hits_ref, live_ref, *refs):
    part_refs, out_ref = refs[:-1], refs[-1]
    capacity = hits_ref.shape[1]
    size = part_refs[0].shape[0] // 2
    rank = size // capacity
    total = sum(ref[...].astype(jnp.float32) for ref in part_refs)
    products = total[:size] * total[size:]
    dense = jnp.zeros((hits_ref.shape[0], products.shape[1]), jnp.float32)
    for slot in range(capacity):
        row = jnp.sum(products[slot * rank : (slot + 1) * rank], axis=0, keepdims=True)
        dense = dense + hits_ref[:, slot : slot + 1] * row
    out_ref[...] = dense * live_ref[...]


def scores_of(hits, live, parts):
    return pl.pallas_call(
        score_kernel,
        out_shape=jax.ShapeDtypeStruct((hits.shape[0], live.shape[1]), jnp.float32),
        name="scores",
    )(hits, live, *parts).T


def spread(pieces, axis):
    return [shifted(piece, axis, distance) for piece, distance in zip(pieces, (1, -1, 2))]


def body(
    hidden_acts,
    layer_inputs,
    norm_gains,
    top_cotangent,
    up_factors,
    down_factors,
    candidates,
    counts,
):
    sections = lax.axis_size("x")
    section, y, z, c = (lax.axis_index(axis) for axis in ("x", "y", "z", "c"))
    me = (y * SIDE + z) * CORES + c
    shards = SIDE * SIDE * CORES
    rows, width = layer_inputs.shape[1:]
    hidden = hidden_acts[0]
    up, down = up_factors[0, 0], down_factors[0, 0]
    rank, ff = up.shape
    up_wide = ff // (2 * SIDE)
    down_wide = width // (2 * SIDE)
    axes, other_axes = ("z", "y"), ("y", "z")
    halves = range(2)

    def stacked(first, pieces):
        blocks = []
        for piece in pieces:
            blocks.append((first, piece, 0, piece.shape[0]))
            first += piece.shape[0]
        return blocks

    def slices(half, sources, wides, rows, steps):
        items = []
        for step in steps:
            to, item = 0, []
            for source, wide in zip(sources, wides):
                item.append((source, (0, rows), 0, to, half * SIDE * wide, wide, axes[half], step))
                to += wide
            items.append(item)
        return items

    queries, listed = candidates.shape
    capacity = listed + listed // 4
    member = jnp.any(
        candidates[:, :, None] == jnp.arange(shards, dtype=jnp.int32)[None, None, :], axis=1
    ).astype(jnp.int32)
    position = jnp.cumsum(member, axis=0) - member
    hits = (
        (member.T[:, None, :] == 1)
        & (position.T[:, None, :] == jnp.arange(capacity, dtype=jnp.int32)[None, :, None])
    )
    query = jnp.arange(queries, dtype=jnp.int32)
    order = jnp.array([0, 2, 3, 1], jnp.int32)
    far_y = order[(query // (CORES * SIDE) - y) % SIDE]
    far_z = order[(query // CORES % SIDE - z) % SIDE]
    other = (query % CORES != c).astype(jnp.int32) * SIDE * SIDE
    kept = (other + far_y * SIDE + far_z, other + far_z * SIDE + far_y)
    where = jnp.concatenate(
        [jnp.sum(jnp.where(hits, place[None, None, :], 0), axis=2) for place in kept]
    )
    own_hits = lax.dynamic_index_in_dim(hits, me, 0, keepdims=False).astype(jnp.float32).T
    live = (jnp.arange(rows, dtype=jnp.int32) < counts[0]).astype(jnp.float32)[None, :]

    outs, token = cut(
        [up, down],
        [
            item
            for half in halves
            for item in slices(half, (0, 1), (up_wide, down_wide), rank, (0, 1, -1, 2))
        ],
        [],
    )
    arrived = [
        outs[half * SIDE : half * SIDE + 1] + spread(outs[half * SIDE + 1 : (half + 1) * SIDE], axes[half])
        for half in halves
    ]
    block = rows // sections
    extra = width // block
    (payload,), token = cut(
        [layer_inputs[0], norm_gains.reshape(block, extra)],
        [
            [
                item
                for part in range(sections)
                for item in (
                    (0, (part * block, block), part * block, 0, 0, width, None, 0),
                    (1, (0, block), part * block, width, 0, extra, None, 0),
                )
            ]
        ],
        [token],
    )
    inputs = lax.all_to_all(payload.reshape(sections, block, -1), "x", 0, 0, tiled=True)
    gains = inputs[:, :, width:].reshape(sections, width)

    near, token = joined([[SIDE * rank] + stacked(0, arrived[half]) for half in halves], [token])
    size = near[0].shape[0]
    before = [shifted(near[half], other_axes[half], 1) for half in halves]
    after = [shifted(near[half], other_axes[half], -1) for half in halves]

    sent, token = cut(
        [hidden],
        [item for half in halves for item in slices(half, (0,), (up_wide,), rows, (1, -1, 2))],
        [token],
        wide=up_wide + down_wide,
    )
    cotangents, token = chain(
        section.reshape(1).astype(jnp.int32),
        inputs,
        gains,
        top_cotangent,
        [token, where, own_hits, live],
    )
    cotangent = lax.all_to_all(cotangents, "x", 0, 0, tiled=True).reshape(rows, width)

    forward, token = joined(
        [
            [size // 2, (0, array, half * size // 2, size // 2)]
            for half in halves
            for array in (before, after)[half]
        ],
        [token],
    )
    far = [
        (shifted(forward[half], other_axes[half], 1), shifted(forward[2 + half], other_axes[half], -1))
        for half in halves
    ]
    ring = SIDE * size
    (mine,), token = joined(
        [
            [2 * ring]
            + [
                block
                for half in halves
                for block in stacked(half * ring, (near[half], before[half], after[half]))
            ]
        ],
        [token],
    )
    def completed(of_half, steps, after):
        return cut(
            [cotangent],
            [item for half in halves for item in slices(half, (0,), (down_wide,), rows, steps)],
            after,
            wide=up_wide + down_wide,
            into=[sent[half * (SIDE - 1) + at] for half in halves for at in of_half],
            start=up_wide,
        )

    beside, token = completed((0, 1), (1, -1), [token])
    (mine,), token = joined(
        [
            [2 * ring]
            + [block for half in halves for block in stacked(half * ring + 3 * size, far[half])]
        ],
        [token],
        into=mine,
    )
    factors = [mine, shifted(mine, "c", 1)]
    farthest, token = completed((2,), (2,), [token, factors[1]])
    arrived = [None, None]
    for half in (1, 0):
        arrived[half] = [
            shifted(beside[2 * half], axes[half], 1),
            shifted(beside[2 * half + 1], axes[half], -1),
        ]
    for half in halves:
        arrived[half].append(shifted(farthest[half], axes[half], 2))

    parts = []
    for plan in (((0, 0), (1, 0), (1, 3), (1, 1)), ((0, 3), (0, 1), (0, 2), (1, 2))):
        tokens = []
        for half, distance in plan:
            if distance == 0:
                tokens.append(((hidden, None), (cotangent, None)))
            else:
                piece = arrived[half][RELATIVE.index(distance) - 1]
                tokens.append(((piece, 0), (piece, up_wide)))
        products, token = project(plan, where, tokens, factors, rank, up_wide, down_wide, [token])
        parts += [
            shifted(product, axes[half], distance) if distance else product
            for product, (half, distance) in zip(products, plan)
        ]
    return scores_of(own_hits, live, parts)[None]


def solution(mesh):
    grid = Mesh(mesh.devices.reshape(-1, SIDE, SIDE, CORES), ("x", "y", "z", "c"))
    dp = ("y", "z", "c")
    return jax.shard_map(
        body,
        mesh=grid,
        in_specs=(
            P("x", dp, None),
            P("x", dp, None),
            P("x", None),
            P(dp, None),
            P(dp, "x", None, None),
            P(dp, "x", None, None),
            P(),
            P(dp),
        ),
        out_specs=P("x", dp, None),
        check_vma=False,
    )
```

```python
import functools

import jax
import jax.numpy as jnp
from jax import lax
from jax.experimental import pallas as pl
from jax.experimental.pallas import tpu as pltpu
from jax.sharding import Mesh
from jax.sharding import PartitionSpec as P

EPSILON = 1e-05
SIDE = 4
CORES = 2
RELATIVE = (0, 3, 1, 2)
ANY = pl.BlockSpec(memory_space=pl.ANY)
SMEM = pl.BlockSpec(memory_space=pltpu.SMEM)
TOKEN = jax.ShapeDtypeStruct((8, 128), jnp.float32)
VMEM_BYTES = 60 << 20


def shifted(block, axis, distance):
    size = lax.axis_size(axis)
    return lax.ppermute(block, axis, [(i, (i + distance) % size) for i in range(size)])


def moved(copies):
    for into, _ in copies:
        for copy in into:
            copy.start()
    for into, out in copies:
        for copy in into:
            copy.wait()
        out.start()
    for _, out in copies:
        out.wait()


def joined_kernel(blocks, arrays, *refs):
    sources, held, sems = refs[:arrays], refs[-2], refs[-1]
    outs = refs[-4 - max(out for out, *_ in blocks) : -3]
    copies, row = [], 0
    for i, (out, to, source, first, rows) in enumerate(blocks):
        here = held.at[pl.ds(row, rows)]
        into = pltpu.make_async_copy(sources[source].at[pl.ds(first, rows)], here, sems.at[0, i])
        copies.append(
            ([into], pltpu.make_async_copy(here, outs[out].at[pl.ds(to, rows)], sems.at[1, i]))
        )
        row += rows
    moved(copies)


def joined(groups, after, into=None):
    arrays, blocks = [], []
    for out, (_, *group) in enumerate(groups):
        for to, array, first, rows in group:
            if not any(array is known for known in arrays):
                arrays.append(array)
            source = [array is known for known in arrays].index(True)
            blocks.append((out, to, source, first, rows))
    wide, dtype = arrays[0].shape[1], arrays[0].dtype
    into = [] if into is None else [into]
    *outs, token = pl.pallas_call(
        functools.partial(joined_kernel, blocks, len(arrays)),
        in_specs=[ANY] * (len(arrays) + len(into) + len(after)),
        out_specs=[ANY] * (len(groups) + 1),
        out_shape=[jax.ShapeDtypeStruct((size, wide), dtype) for size, *_ in groups] + [TOKEN],
        scratch_shapes=[
            pltpu.VMEM((sum(block[-1] for block in blocks), wide), dtype),
            pltpu.SemaphoreType.DMA((2, len(blocks))),
        ],
        input_output_aliases={len(arrays) + i: i for i in range(len(into))},
        compiler_params=pltpu.CompilerParams(vmem_limit_bytes=VMEM_BYTES),
        name="joined",
    )(*arrays, *into, *after)
    return outs, token


def cut_kernel(plan, arrays, starts, *refs):
    sources = refs[:arrays]
    count = len(plan)
    outs, held, sems = refs[-2 - 2 * count : -2 - count], refs[-1 - count : -1], refs[-1]
    copies = []
    for at, (sources_of, out_ref, buffer) in enumerate(zip(plan, outs, held)):
        into = []
        for source, rows, to_row, to, first, wide, by, step in sources_of:
            start = first
            if by is not None:
                start = pl.multiple_of(first + (lax.axis_index(by) + step) % SIDE * wide, 128)
            into.append(
                pltpu.make_async_copy(
                    sources[source].at[pl.ds(*rows), pl.ds(start, wide)],
                    buffer.at[pl.ds(to_row, rows[1]), pl.ds(to, wide)],
                    sems.at[at, len(into)],
                )
            )
        target = out_ref.at[:, pl.ds(starts[at], buffer.shape[1])]
        copies.append((into, pltpu.make_async_copy(buffer, target, sems.at[at, len(into)])))
    moved(copies)


def cut(arrays, plan, after, wide=None, into=None, start=0):
    shapes = [
        (max(to_row + rows[1] for _, rows, to_row, *_ in item), max(to + columns for _, _, _, to, _, columns, *_ in item))
        for item in plan
    ]
    dtype = arrays[0].dtype
    into = into or []
    *outs, token = pl.pallas_call(
        functools.partial(cut_kernel, plan, len(arrays), [start] * len(plan)),
        in_specs=[ANY] * (len(arrays) + len(into) + len(after)),
        out_specs=[ANY] * (len(plan) + 1),
        out_shape=[jax.ShapeDtypeStruct((shape[0], wide or shape[1]), dtype) for shape in shapes]
        + [TOKEN],
        scratch_shapes=[pltpu.VMEM(shape, dtype) for shape in shapes]
        + [pltpu.SemaphoreType.DMA((len(plan), 1 + max(len(item) for item in plan)))],
        input_output_aliases={len(arrays) + i: i for i in range(len(into))},
        compiler_params=pltpu.CompilerParams(vmem_limit_bytes=VMEM_BYTES),
        name="cut",
    )(*arrays, *into, *after)
    return outs, token


def payload_kernel(sections, inputs_ref, gains_ref, *refs):
    out_ref, _, held, sems = refs[-4:]
    rows, width = inputs_ref.shape
    block = rows // sections
    extra = width // block
    into = pltpu.make_async_copy(inputs_ref, held.at[:, pl.ds(0, width)], sems.at[0])
    into.start()
    gains = gains_ref[...].astype(jnp.float32)
    folded = jnp.concatenate(
        [gains[:, row * extra : (row + 1) * extra] for row in range(block)], axis=0
    ).astype(held.dtype)
    for part in range(sections):
        held[part * block : (part + 1) * block, width:] = folded
    into.wait()
    out = pltpu.make_async_copy(held, out_ref, sems.at[1])
    out.start()
    out.wait()


def payload_of(inputs, gains, sections, after):
    rows, width = inputs.shape
    out = jax.ShapeDtypeStruct((rows, width + width * sections // rows), inputs.dtype)
    return pl.pallas_call(
        functools.partial(payload_kernel, sections),
        in_specs=[ANY, pl.BlockSpec(memory_space=pltpu.VMEM)] + [ANY] * len(after),
        out_specs=[ANY, ANY],
        out_shape=[out, TOKEN],
        scratch_shapes=[pltpu.VMEM(out.shape, out.dtype), pltpu.SemaphoreType.DMA((2,))],
        compiler_params=pltpu.CompilerParams(vmem_limit_bytes=VMEM_BYTES),
        name="payload",
    )(inputs, gains, *after)


def chain_kernel(section_ref, inputs_ref, gains_ref, top_ref, *refs):
    out_ref = refs[-2]
    sections, width = inputs_ref.shape[0], top_ref.shape[1]
    cotangent = top_ref[...].astype(jnp.float32)
    out_ref[sections - 1] = top_ref[...]
    for layer in range(sections - 1, 0, -1):
        gain = gains_ref[layer : layer + 1, :].astype(jnp.float32)
        values = inputs_ref[layer, :, :width].astype(jnp.float32)
        inverse = lax.rsqrt(jnp.mean(values * values, axis=-1, keepdims=True) + EPSILON)
        normed = values * inverse
        scaled = gain * cotangent
        pulled = jnp.mean(normed * scaled, axis=-1, keepdims=True)
        cotangent = cotangent + scaled * inverse - normed * inverse * pulled
        out_ref[layer - 1] = cotangent.astype(out_ref.dtype)


def chain(section, inputs, gains, top, after):
    sections, rows, wide_in = inputs.shape
    width = top.shape[1]
    step = 16
    steps = rows // step
    return pl.pallas_call(
        chain_kernel,
        grid_spec=pltpu.PrefetchScalarGridSpec(
            num_scalar_prefetch=1,
            grid=(steps,),
            in_specs=[
                pl.BlockSpec((sections, step, wide_in), lambda i, section_ref: (0, i, 0)),
                pl.BlockSpec((sections, width), lambda i, section_ref: (0, 0)),
                pl.BlockSpec((step, width), lambda i, section_ref: (section_ref[0] * steps + i, 0)),
            ]
            + [ANY] * len(after),
            out_specs=[
                pl.BlockSpec((sections, step, width), lambda i, section_ref: (0, i, 0)),
                ANY,
            ],
        ),
        out_shape=[jax.ShapeDtypeStruct((sections, rows, width), jnp.bfloat16), TOKEN],
        compiler_params=pltpu.CompilerParams(vmem_limit_bytes=VMEM_BYTES),
        name="cotangent_chain",
    )(section, inputs, gains, top, *after)


def project_kernel(plan, sources, up_wide, down_wide, where_ref, *refs):
    pieces = len(plan)
    factor_refs, token_refs = refs[:CORES], refs[CORES:]
    outs = refs[-4 - pieces : -4]
    factor_ref, token_ref, sems = refs[-3:]
    capacity = where_ref.shape[1]
    rank = factor_ref.shape[1] // capacity
    halves = 2
    y, z, c = (lax.axis_index(axis) for axis in ("y", "z", "c"))
    wides = up_wide, down_wide

    def place_of(piece):
        half, distance = plan[piece]
        return ((y if half else z) + distance) % SIDE

    def row_of(piece):
        half, _ = plan[piece]
        place = place_of(piece)
        shard = (place * SIDE + z) * CORES + c if half else (y * SIDE + place) * CORES + c
        return half * (where_ref.shape[0] // halves) + shard

    def slot_copy(source, row, piece, slot):
        return pltpu.make_async_copy(
            source.at[pl.ds(pl.multiple_of(row * rank, rank), rank)],
            factor_ref.at[piece, pl.ds(slot * rank, rank)],
            sems.at[piece, slot],
        )

    def token_copies(piece):
        to, copies = 0, []
        for part, wide in enumerate(wides):
            source, column = sources[piece][part]
            if column is None:
                column = pl.multiple_of((plan[piece][0] * SIDE + place_of(piece)) * wide, 128)
            copies.append(
                pltpu.make_async_copy(
                    token_refs[source].at[:, pl.ds(column, wide)],
                    token_ref.at[piece, :, pl.ds(to, wide)],
                    sems.at[piece, capacity + part],
                )
            )
            to += wide
        return copies

    groups = 2
    slots = capacity // groups
    chunks = [(piece, group) for piece in range(pieces) for group in range(groups)]

    def begin(piece, group):
        half, _ = plan[piece]
        if group == 0:
            for copy in token_copies(piece):
                copy.start()
        listed = row_of(piece)
        held = SIDE * SIDE
        for slot in range(group * slots, (group + 1) * slots):
            row = where_ref[listed, slot]
            for core, source in enumerate(factor_refs):

                @pl.when(row // held == core)
                def _(source=source, row=half * held + row % held, slot=slot, piece=piece):
                    slot_copy(source, row, piece, slot).start()

    size = capacity * rank
    ahead = 2
    for chunk in chunks[:ahead]:
        begin(*chunk)
    for at, (piece, group) in enumerate(chunks):
        if group == 0:
            for copy in token_copies(piece):
                copy.wait()
        for slot in range(group * slots, (group + 1) * slots):
            slot_copy(factor_refs[0], 0, piece, slot).wait()
        if at + ahead < len(chunks):
            begin(*chunks[at + ahead])
        first, last = group * slots * rank, (group + 1) * slots * rank
        for side, columns in enumerate((slice(0, up_wide), slice(up_wide, up_wide + down_wide))):
            part = lax.dot_general(
                factor_ref[piece, first:last, columns],
                token_ref[piece, :, columns],
                (((1,), (1,)), ((), ())),
                preferred_element_type=jnp.float32,
            )
            outs[piece][side * size + first : side * size + last] = part.astype(outs[piece].dtype)


def project(plan, where, tokens, factors, rank, up_wide, down_wide, after):
    pieces, capacity = len(plan), where.shape[1]
    rows = tokens[0][0][0].shape[0]
    arrays = []
    sources = []
    for pair in tokens:
        for array, _ in pair:
            if not any(array is known for known in arrays):
                arrays.append(array)
        sources.append(
            [([array is known for known in arrays].index(True), column) for array, column in pair]
        )
    vmem = pl.BlockSpec(memory_space=pltpu.VMEM)
    *outs, token = pl.pallas_call(
        functools.partial(project_kernel, plan, sources, up_wide, down_wide),
        in_specs=[SMEM] + [ANY] * (len(factors) + len(arrays) + len(after)),
        out_specs=[vmem] * pieces + [ANY],
        out_shape=[
            jax.ShapeDtypeStruct(
                (2 * capacity * rank, rows), jnp.bfloat16 if distance else jnp.float32
            )
            for _, distance in plan
        ]
        + [TOKEN],
        scratch_shapes=[
            pltpu.VMEM((pieces, capacity * rank, up_wide + down_wide), jnp.bfloat16),
            pltpu.VMEM((pieces, rows, up_wide + down_wide), jnp.bfloat16),
            pltpu.SemaphoreType.DMA((pieces, capacity + 2)),
        ],
        compiler_params=pltpu.CompilerParams(vmem_limit_bytes=VMEM_BYTES),
        name="project",
    )(where, *factors, *arrays, *after)
    return outs, token


def score_kernel(hits_ref, live_ref, *refs):
    part_refs, out_ref = refs[:-1], refs[-1]
    capacity = hits_ref.shape[1]
    size = part_refs[0].shape[0] // 2
    rank = size // capacity
    total = sum(ref[...].astype(jnp.float32) for ref in part_refs)
    products = total[:size] * total[size:]
    dense = jnp.zeros((hits_ref.shape[0], products.shape[1]), jnp.float32)
    for slot in range(capacity):
        row = jnp.sum(products[slot * rank : (slot + 1) * rank], axis=0, keepdims=True)
        dense = dense + hits_ref[:, slot : slot + 1] * row
    out_ref[...] = dense * live_ref[...]


def scores_of(hits, live, parts):
    return pl.pallas_call(
        score_kernel,
        out_shape=jax.ShapeDtypeStruct((hits.shape[0], live.shape[1]), jnp.float32),
        name="scores",
    )(hits, live, *parts).T


def spread(pieces, axis):
    return [shifted(piece, axis, distance) for piece, distance in zip(pieces, (1, -1, 2))]


def body(
    hidden_acts,
    layer_inputs,
    norm_gains,
    top_cotangent,
    up_factors,
    down_factors,
    candidates,
    counts,
):
    sections = lax.axis_size("x")
    section, y, z, c = (lax.axis_index(axis) for axis in ("x", "y", "z", "c"))
    me = (y * SIDE + z) * CORES + c
    shards = SIDE * SIDE * CORES
    rows, width = layer_inputs.shape[1:]
    hidden = hidden_acts[0]
    up, down = up_factors[0, 0], down_factors[0, 0]
    rank, ff = up.shape
    up_wide = ff // (2 * SIDE)
    down_wide = width // (2 * SIDE)
    axes, other_axes = ("z", "y"), ("y", "z")
    halves = range(2)

    def stacked(first, pieces):
        blocks = []
        for piece in pieces:
            blocks.append((first, piece, 0, piece.shape[0]))
            first += piece.shape[0]
        return blocks

    def slices(half, sources, wides, rows, steps):
        items = []
        for step in steps:
            to, item = 0, []
            for source, wide in zip(sources, wides):
                item.append((source, (0, rows), 0, to, half * SIDE * wide, wide, axes[half], step))
                to += wide
            items.append(item)
        return items

    queries, listed = candidates.shape
    capacity = listed + listed // 4
    member = jnp.any(
        candidates[:, :, None] == jnp.arange(shards, dtype=jnp.int32)[None, None, :], axis=1
    ).astype(jnp.int32)
    position = jnp.cumsum(member, axis=0) - member
    hits = (
        (member.T[:, None, :] == 1)
        & (position.T[:, None, :] == jnp.arange(capacity, dtype=jnp.int32)[None, :, None])
    )
    query = jnp.arange(queries, dtype=jnp.int32)
    order = jnp.array([0, 2, 3, 1], jnp.int32)
    far_y = order[(query // (CORES * SIDE) - y) % SIDE]
    far_z = order[(query // CORES % SIDE - z) % SIDE]
    other = (query % CORES != c).astype(jnp.int32) * SIDE * SIDE
    kept = (other + far_y * SIDE + far_z, other + far_z * SIDE + far_y)
    where = jnp.concatenate(
        [jnp.sum(jnp.where(hits, place[None, None, :], 0), axis=2) for place in kept]
    )
    own_hits = lax.dynamic_index_in_dim(hits, me, 0, keepdims=False).astype(jnp.float32).T
    live = (jnp.arange(rows, dtype=jnp.int32) < counts[0]).astype(jnp.float32)[None, :]

    outs, token = cut(
        [up, down],
        [
            item
            for half in halves
            for item in slices(half, (0, 1), (up_wide, down_wide), rank, (0, 1, -1, 2))
        ],
        [],
    )
    opposite = [shifted(outs[half * SIDE + 3], axes[half], 2) for half in halves]
    arrived = [
        [
            outs[half * SIDE],
            shifted(outs[half * SIDE + 1], axes[half], 1),
            shifted(outs[half * SIDE + 2], axes[half], -1),
            opposite[half],
        ]
        for half in halves
    ]
    block = rows // sections
    payload, token = payload_of(layer_inputs[0], norm_gains, sections, [token])
    inputs = lax.all_to_all(payload.reshape(sections, block, -1), "x", 0, 0, tiled=True)
    gains = inputs[:, :, width:].reshape(sections, width)

    near, token = joined([[SIDE * rank] + stacked(0, arrived[half]) for half in halves], [token])
    size = near[0].shape[0]
    before = [shifted(near[half], other_axes[half], 1) for half in halves]
    after = [shifted(near[half], other_axes[half], -1) for half in halves]

    sent, token = cut(
        [hidden],
        [item for half in halves for item in slices(half, (0,), (up_wide,), rows, (1, -1, 2))],
        [token],
        wide=up_wide + down_wide,
    )
    cotangents, token = chain(
        section.reshape(1).astype(jnp.int32),
        inputs,
        gains,
        top_cotangent,
        [token, where, own_hits, live],
    )
    cotangent = lax.all_to_all(cotangents, "x", 0, 0, tiled=True).reshape(rows, width)

    forward, token = joined(
        [
            [size // 2, (0, array, half * size // 2, size // 2)]
            for half in halves
            for array in (before, after)[half]
        ],
        [token],
    )
    far = [
        (shifted(forward[half], other_axes[half], 1), shifted(forward[2 + half], other_axes[half], -1))
        for half in halves
    ]
    ring = SIDE * size
    (mine,), token = joined(
        [
            [2 * ring]
            + [
                block
                for half in halves
                for block in stacked(half * ring, (near[half], before[half], after[half]))
            ]
        ],
        [token],
    )
    def completed(of_half, steps, after):
        return cut(
            [cotangent],
            [item for half in halves for item in slices(half, (0,), (down_wide,), rows, steps)],
            after,
            wide=up_wide + down_wide,
            into=[sent[half * (SIDE - 1) + at] for half in halves for at in of_half],
            start=up_wide,
        )

    beside, token = completed((0, 1), (1, -1), [token])
    (mine,), token = joined(
        [
            [2 * ring]
            + [block for half in halves for block in stacked(half * ring + 3 * size, far[half])]
        ],
        [token],
        into=mine,
    )
    factors = [mine, shifted(mine, "c", 1)]
    farthest, token = completed((2,), (2,), [token, factors[1]])
    arrived = [None, None]
    for half in (1, 0):
        arrived[half] = [
            shifted(beside[2 * half], axes[half], 1),
            shifted(beside[2 * half + 1], axes[half], -1),
        ]
    for half in halves:
        arrived[half].append(shifted(farthest[half], axes[half], 2))

    parts = []
    for plan in (((0, 0), (1, 0), (1, 3), (1, 1)), ((0, 3), (0, 1), (0, 2), (1, 2))):
        tokens = []
        for half, distance in plan:
            if distance == 0:
                tokens.append(((hidden, None), (cotangent, None)))
            else:
                piece = arrived[half][RELATIVE.index(distance) - 1]
                tokens.append(((piece, 0), (piece, up_wide)))
        products, token = project(plan, where, tokens, factors, rank, up_wide, down_wide, [token])
        parts += [
            shifted(product, axes[half], distance) if distance else product
            for product, (half, distance) in zip(products, plan)
        ]
    return scores_of(own_hits, live, parts)[None]


def solution(mesh):
    grid = Mesh(mesh.devices.reshape(-1, SIDE, SIDE, CORES), ("x", "y", "z", "c"))
    dp = ("y", "z", "c")
    return jax.shard_map(
        body,
        mesh=grid,
        in_specs=(
            P("x", dp, None),
            P("x", dp, None),
            P("x", None),
            P(dp, None),
            P(dp, "x", None, None),
            P(dp, "x", None, None),
            P(),
            P(dp),
        ),
        out_specs=P("x", dp, None),
        check_vma=False,
    )
```
